128 devices in a mesh: uly: 8 (over z, x_hi), blk: 16 (over x_lo, y, core).
Axes of the slice: x: 4 (x_hi: 2, x_lo: 2; x = x_hi * 2 + x_lo), y: 4, z: 4, core: 2. Of those that a mesh axis runs over, the one named last changes fastest.
Arguments:
- queries: bfloat16 [1, 12288, 3072], P(None, ('uly', 'blk')), may hold values from -26 to 26
- key_states: bfloat16 [1, 12288, 3072], P(None, ('uly', 'blk')), may hold values from -16 to 16
- value_states: bfloat16 [1, 12288, 3072], P(None, ('uly', 'blk')), may hold values from -6 to 6
Outputs:
- attended: bfloat16 [1, 12288, 3072], P(None, ('uly', 'blk'))
The draws below stay inside these ranges and needn't reach their ends.
All inputs are finite; a program needn't handle non-finite values.
Results may differ from the reference program's by a relative error of at most 0.0055.
Values may be sent and summed in bfloat16 or wider, within the bound.
No kernel may reach another device: no remote copies, remote signals or barrier semaphores. Data moves between devices by JAX's collectives and lax.ppermute only.
A program may use at most 128 MiB of HBM per device.

```python
import math
import jax
import jax.numpy as jnp
from jax import lax

HEADS = 24
HEAD = 128
SEQS = 1
LEN = 12288


def key_field(key, normal_part):
    first = jax.random.fold_in(key, 41)
    shape = (SEQS * LEN, HEADS * HEAD)
    normal_values = jnp.clip(normal_part * jax.random.normal(first, shape, jnp.float32), -16.0, 16.0)
    return normal_values


def draw_key_states(key, part):
    flat = key_field(key, 2.0)
    return flat.reshape(SEQS, LEN, HEADS * HEAD).astype(jnp.bfloat16)


def draw_queries(key, part):
    own = jax.random.fold_in(key, 5)
    flat = jnp.clip(2.0 * jax.random.normal(own, (SEQS * LEN, HEADS * HEAD), jnp.float32), -16.0, 16.0)
    return flat.reshape(SEQS, LEN, HEADS * HEAD).astype(jnp.bfloat16)


def block_scale(key, dims, cuts, smallest, high):
    def one(axis_at, blocks):
        steps = jax.random.uniform(jax.random.fold_in(jax.random.fold_in(key, 6), axis_at), (blocks,), jnp.float32, smallest / len(cuts), high / len(cuts))
        return jnp.repeat(jnp.exp(steps), dims[axis_at] // blocks).reshape((-1,) + (1,) * (len(dims) - axis_at - 1))

    gain = one(*cuts[0])
    for cut in cuts[1:]:
        gain = gain * one(*cut)
    return gain


def bell_draw(key, shape, scale, most, split=(), kind=jnp.bfloat16):
    gain = block_scale(key, shape, split, -0.22, 0.18) if split else 1.0
    values = jax.random.normal(key, shape, jnp.float32) * scale * gain
    return jnp.minimum(jnp.maximum(values, -most), most).astype(kind)


def setup_inputs(seed: int = 0) -> dict:
    key_of = jax.random.split(jax.random.key(seed), 4)
    return {
        "queries": draw_queries(jax.random.fold_in(key_of[3], 71), 0),
        "key_states": draw_key_states(jax.random.fold_in(key_of[3], 71), 0),
        "value_states": bell_draw(key_of[2], (SEQS, LEN, HEADS * HEAD), 1.0, 6.0, ((1, 128),)),
    }


def head_attention(query_head, key_head, value_head):
    length = query_head.shape[0]
    block_rows = math.gcd(length, 1024)
    blocks = query_head.reshape(length // block_rows, block_rows, query_head.shape[1])
    score_scale = 1.0 / math.sqrt(HEAD)

    def one_block(query_block):
        scores = jnp.dot(query_block, key_head.T, preferred_element_type=jnp.float32) * score_scale
        row_max = lax.optimization_barrier(jnp.max(scores, axis=1, keepdims=True))
        weights = jnp.exp(scores - row_max)
        row_sum = lax.optimization_barrier(jnp.sum(weights, axis=1, keepdims=True))
        mixed = jnp.dot(weights.astype(jnp.bfloat16), value_head, preferred_element_type=jnp.float32)
        return (mixed / row_sum).astype(jnp.bfloat16)
    return lax.map(one_block, blocks).reshape(length, value_head.shape[1])

def reference(queries, key_states, value_states):
    seq_count, length, feature_width = queries.shape
    head_count = feature_width // HEAD

    def split_heads(array):
        shaped = array.reshape(seq_count, length, head_count, HEAD).transpose(0, 2, 1, 3)
        return shaped.reshape(seq_count * head_count, length, HEAD)
    result = lax.map(lambda trio: head_attention(trio[0], trio[1], trio[2]), (split_heads(queries), split_heads(key_states), split_heads(value_states)))
    result = result.reshape(seq_count, head_count, length, HEAD).transpose(0, 2, 1, 3)
    return result.reshape(seq_count, length, feature_width)
```

```python
import functools
import math

import jax
import jax.numpy as jnp
from jax import lax
from jax.experimental import pallas as pl
from jax.experimental.pallas import tpu as pltpu
from jax.sharding import Mesh
from jax.sharding import PartitionSpec as P

HEAD = 128
HEADS_HERE = 3
WIDTH = HEAD * HEADS_HERE
GROUPS = 8
TOKENS = 96
ROWS = GROUPS * TOKENS
STAT_ROWS = 32
SENT_ROWS = ROWS + STAT_ROWS
SUB_ROWS = 256
SCALE = math.log2(math.e) / math.sqrt(HEAD)
ULY = ("z", "xh")
VMEM = 20 * 2**20


def regroup_kernel(q_ref, k_ref, v_ref, out_ref):
    for g in range(GROUPS):
        for part, ref in enumerate((q_ref, k_ref, v_ref)):
            out_ref[g, :, part * WIDTH : (part + 1) * WIDTH] = ref[:, g * WIDTH : (g + 1) * WIDTH]


def regroup(queries, keys, values):
    whole = pl.BlockSpec(memory_space=pltpu.VMEM)
    return pl.pallas_call(
        regroup_kernel,
        in_specs=[whole] * 3,
        out_specs=whole,
        out_shape=jax.ShapeDtypeStruct((GROUPS, TOKENS, 3 * WIDTH), queries.dtype),
        compiler_params=pltpu.CompilerParams(vmem_limit_bytes=VMEM),
    )(queries, keys, values)


def ungroup_kernel(in_ref, out_ref):
    for g in range(GROUPS):
        out_ref[:, g * WIDTH : (g + 1) * WIDTH] = in_ref[g]


def ungroup(parts):
    whole = pl.BlockSpec(memory_space=pltpu.VMEM)
    return pl.pallas_call(
        ungroup_kernel,
        in_specs=[whole],
        out_specs=whole,
        out_shape=jax.ShapeDtypeStruct((TOKENS, GROUPS * WIDTH), parts.dtype),
        compiler_params=pltpu.CompilerParams(vmem_limit_bytes=VMEM),
    )(parts)


def diagonal():
    rows = lax.broadcasted_iota(jnp.int32, (HEAD, HEAD), 0)
    cols = lax.broadcasted_iota(jnp.int32, (HEAD, HEAD), 1)
    return rows == cols


def across(column, width):
    return jnp.concatenate([column] * (width // HEAD), axis=1)


def attend_kernel(*refs, firsts, resumed, final):
    q_ref = refs[0]
    sources = len(firsts)
    state_ref = refs[1 + sources] if resumed else None
    out_ref = refs[-1]
    tiles = ROWS // SUB_ROWS
    jobs = [(h, t, s) for h in range(HEADS_HERE) for t in range(tiles) for s in range(sources)]
    ones = jnp.ones((ROWS, HEAD), jnp.bfloat16)

    def columns(s, which, h):
        at = firsts[s] + which * WIDTH + h * HEAD
        return refs[1 + s][:, at : at + HEAD]

    def scores_of(h, t, s):
        return lax.dot_general(
            q_ref[t * SUB_ROWS : (t + 1) * SUB_ROWS, h * HEAD : (h + 1) * HEAD],
            columns(s, 0, h),
            (((1,), (1,)), ((), ())),
            preferred_element_type=jnp.float32,
        )

    top = total = None
    logs = []
    scores = scores_of(*jobs[0])
    for n, (h, t, s) in enumerate(jobs):
        upcoming = scores_of(*jobs[n + 1]) if n + 1 < len(jobs) else None
        at = slice(t * SUB_ROWS, (t + 1) * SUB_ROWS)
        mine = slice(h * HEAD, (h + 1) * HEAD)
        if s == 0 and resumed:
            total = state_ref[h, at, : 2 * HEAD]
            top = state_ref[h, at, 2 * HEAD :]
        first = s == 0 and not resumed
        high = jnp.max(scores, axis=1, keepdims=True) * SCALE
        high = jnp.broadcast_to(high, (SUB_ROWS, HEAD))
        if not first:
            high = jnp.maximum(top, high)
        weights = jnp.exp2(scores * SCALE - across(high, ROWS)).astype(jnp.bfloat16)
        widened = jnp.concatenate([columns(s, 1, h), ones], axis=1)
        product = jnp.dot(weights, widened, preferred_element_type=jnp.float32)
        if not first:
            product = product + total * across(jnp.exp2(top - high), 2 * HEAD)
        top, total = high, product
        if s == sources - 1:
            if final:
                row_sum = total[:, HEAD:]
                out_ref[at, mine] = (total[:, :HEAD] / row_sum).astype(out_ref.dtype)
                logs.append(top + jnp.log2(row_sum))
            else:
                out_ref[h, at, : 2 * HEAD] = total
                out_ref[h, at, 2 * HEAD :] = top
        scores = upcoming
        if final and s == sources - 1 and t == tiles - 1:
            eye = diagonal()
            lines = []
            for log in logs:
                for g in range(SUB_ROWS // HEAD):
                    piece = log[g * HEAD : (g + 1) * HEAD]
                    lines.append(jnp.sum(jnp.where(eye, piece, 0.0), axis=0, keepdims=True))
            lines.append(jnp.zeros((8 - len(lines), HEAD), jnp.float32))
            whole = jnp.concatenate(lines, axis=0)
            part1 = whole.astype(jnp.bfloat16)
            rest = whole - part1.astype(jnp.float32)
            part2 = rest.astype(jnp.bfloat16)
            part3 = (rest - part2.astype(jnp.float32)).astype(jnp.bfloat16)
            out_ref[ROWS:, mine] = jnp.concatenate(
                [part1, part2, part3, jnp.zeros((8, HEAD), jnp.bfloat16)], axis=0
            )
            logs = []


def attend(queries, sources, state=None, final=False):
    whole = pl.BlockSpec(memory_space=pltpu.VMEM)
    operands = [queries] + [array for array, _ in sources]
    if state is not None:
        operands.append(state)
    if final:
        out_shape = jax.ShapeDtypeStruct((SENT_ROWS, WIDTH), jnp.bfloat16)
    else:
        out_shape = jax.ShapeDtypeStruct((HEADS_HERE, ROWS, 3 * HEAD), jnp.float32)
    return pl.pallas_call(
        functools.partial(
            attend_kernel,
            firsts=[first for _, first in sources],
            resumed=state is not None,
            final=final,
        ),
        in_specs=[whole] * len(operands),
        out_specs=whole,
        out_shape=out_shape,
        compiler_params=pltpu.CompilerParams(vmem_limit_bytes=VMEM),
        cost_estimate=pl.CostEstimate(flops=1, bytes_accessed=1, transcendentals=0),
    )(*operands)


def merge_kernel(*refs):
    *parts, out_ref = refs
    logs = []
    for part in parts:
        stats = part[ROWS:, :].astype(jnp.float32)
        logs.append(stats[0:8] + (stats[8:16] + stats[16:24]))
    high = functools.reduce(jnp.maximum, logs)
    shares = [jnp.exp2(log - high) for log in logs]
    whole = functools.reduce(jnp.add, shares)
    shares = [share / whole for share in shares]
    eye = diagonal()
    ones = jnp.ones((2 * HEAD, HEAD), jnp.bfloat16)
    for h in range(HEADS_HERE):
        mine = slice(h * HEAD, (h + 1) * HEAD)
        for g in range(ROWS // HEAD):
            at = slice(g * HEAD, (g + 1) * HEAD)
            total = None
            for part, share in zip(parts, shares):
                spread = jnp.where(eye, share[g : g + 1, mine], 0.0)
                coarse = spread.astype(jnp.bfloat16)
                fine = (spread - coarse.astype(jnp.float32)).astype(jnp.bfloat16)
                column = jnp.dot(
                    jnp.concatenate([coarse, fine], axis=1),
                    ones,
                    preferred_element_type=jnp.float32,
                )
                term = part[at, mine].astype(jnp.float32) * column
                total = term if total is None else total + term
            out_ref[at, mine] = total.astype(out_ref.dtype)


def merge(parts):
    return pl.pallas_call(
        merge_kernel,
        in_specs=[pl.BlockSpec(memory_space=pltpu.VMEM)] * len(parts),
        out_specs=pl.BlockSpec(memory_space=pltpu.VMEM),
        out_shape=jax.ShapeDtypeStruct((ROWS, WIDTH), jnp.bfloat16),
        cost_estimate=pl.CostEstimate(flops=1, bytes_accessed=1, transcendentals=0),
    )(*parts)


def shift(array, axis, count, step):
    return lax.ppermute(array, axis, [(i, (i + step) % count) for i in range(count)])


def per_device(queries, key_states, value_states):
    grouped = regroup(queries[0], key_states[0], value_states[0])
    own = lax.all_to_all(grouped, ULY, 0, 0).reshape(ROWS, 3 * WIDTH)
    own_q, own_kv = own[:, :WIDTH], own[:, WIDTH:]

    core_kv = shift(own_kv, "c", 2, 1)
    side_kv = shift(own_kv, "xl", 2, 1)
    q_up = shift(own_q, "y", 4, 1)
    q_down = shift(own_q, "y", 4, -1)
    q_far = shift(own_q, "y", 4, 2)

    near = [(own, WIDTH), (core_kv, 0)]
    state_own = attend(own, near)
    q_up, state_own = lax.optimization_barrier((q_up, state_own))
    state_up = attend(q_up, near)
    q_down, state_up = lax.optimization_barrier((q_down, state_up))
    state_down = attend(q_down, near)
    side_kv, state_down = lax.optimization_barrier((side_kv, state_down))
    side_core_kv = shift(side_kv, "c", 2, 1)
    side = [(side_kv, 0), (side_core_kv, 0)]

    far = shift(attend(q_far, near + side, final=True), "y", 4, 2)
    up = shift(attend(q_up, side, state_up, final=True), "y", 4, -1)
    down = shift(attend(q_down, side, state_down, final=True), "y", 4, 1)
    mine = attend(own, side, state_own, final=True)

    merged = merge([mine, up, down, far]).reshape(GROUPS, TOKENS, WIDTH)
    return ungroup(lax.all_to_all(merged, ULY, 0, 0))[None]


def solution(mesh):
    split = Mesh(mesh.devices.reshape(4, 2, 2, 4, 2), ("z", "xh", "xl", "y", "c"))
    placed = P(None, ("z", "xh", "xl", "y", "c"), None)
    return jax.shard_map(
        per_device,
        mesh=split,
        in_specs=(placed, placed, placed),
        out_specs=placed,
        check_vma=False,
    )
```

```python
import functools
import math

import jax
import jax.numpy as jnp
from jax import lax
from jax.experimental import pallas as pl
from jax.experimental.pallas import tpu as pltpu
from jax.sharding import Mesh
from jax.sharding import PartitionSpec as P

HEAD = 128
HEADS_HERE = 3
WIDTH = HEAD * HEADS_HERE
GROUPS = 8
TOKENS = 96
ROWS = GROUPS * TOKENS
STAT_ROWS = 32
SENT_ROWS = ROWS + STAT_ROWS
SUB_ROWS = 256
SCALE = math.log2(math.e) / math.sqrt(HEAD)
ULY = ("z", "xh")
VMEM = 20 * 2**20


def regroup_kernel(*refs):
    count = (len(refs) - 2) // 2
    in_refs, out_ref, held, sems = refs[:count], refs[count], refs[count + 1 : -1], refs[-1]
    copies = [
        pltpu.make_async_copy(ref, block, sems.at[part])
        for part, (ref, block) in enumerate(zip(in_refs, held))
    ]
    for copy in copies:
        copy.start()
    for part, (copy, block) in enumerate(zip(copies, held)):
        copy.wait()
        for g in range(GROUPS):
            out_ref[g, :, part * WIDTH : (part + 1) * WIDTH] = block[:, g * WIDTH : (g + 1) * WIDTH]


def regroup(*arrays):
    return pl.pallas_call(
        regroup_kernel,
        in_specs=[pl.BlockSpec(memory_space=pl.ANY)] * len(arrays),
        out_specs=pl.BlockSpec(memory_space=pltpu.VMEM),
        out_shape=jax.ShapeDtypeStruct((GROUPS, TOKENS, len(arrays) * WIDTH), arrays[0].dtype),
        scratch_shapes=[pltpu.VMEM(array.shape, array.dtype) for array in arrays]
        + [pltpu.SemaphoreType.DMA((len(arrays),))],
        compiler_params=pltpu.CompilerParams(vmem_limit_bytes=VMEM),
    )(*arrays)


def ungroup_kernel(in_ref, out_ref):
    for g in range(GROUPS):
        out_ref[:, g * WIDTH : (g + 1) * WIDTH] = in_ref[g]


def ungroup(parts):
    whole = pl.BlockSpec(memory_space=pltpu.VMEM)
    return pl.pallas_call(
        ungroup_kernel,
        in_specs=[whole],
        out_specs=whole,
        out_shape=jax.ShapeDtypeStruct((TOKENS, GROUPS * WIDTH), parts.dtype),
        compiler_params=pltpu.CompilerParams(vmem_limit_bytes=VMEM),
    )(parts)


def diagonal():
    rows = lax.broadcasted_iota(jnp.int32, (HEAD, HEAD), 0)
    cols = lax.broadcasted_iota(jnp.int32, (HEAD, HEAD), 1)
    return rows == cols


def across(column, width):
    return jnp.concatenate([column] * (width // HEAD), axis=1)


def attend_kernel(*refs, places, resumed, final):
    q_ref = refs[0]
    sources = len(places)
    state_ref = refs[-2] if resumed else None
    out_ref = refs[-1]
    tiles = ROWS // SUB_ROWS
    jobs = [(h, t, s) for h in range(HEADS_HERE) for t in range(tiles) for s in range(sources)]
    ones = jnp.ones((ROWS, HEAD), jnp.bfloat16)

    def columns(s, which, h):
        ref, first = places[s][which]
        at = first + h * HEAD
        return refs[ref][:, at : at + HEAD]

    def scores_of(h, t, s):
        return lax.dot_general(
            q_ref[t * SUB_ROWS : (t + 1) * SUB_ROWS, h * HEAD : (h + 1) * HEAD],
            columns(s, 0, h),
            (((1,), (1,)), ((), ())),
            preferred_element_type=jnp.float32,
        )

    top = total = None
    logs = []
    scores = scores_of(*jobs[0])
    for n, (h, t, s) in enumerate(jobs):
        upcoming = scores_of(*jobs[n + 1]) if n + 1 < len(jobs) else None
        at = slice(t * SUB_ROWS, (t + 1) * SUB_ROWS)
        mine = slice(h * HEAD, (h + 1) * HEAD)
        if s == 0 and resumed:
            total = state_ref[h, at, : 2 * HEAD]
            top = state_ref[h, at, 2 * HEAD :]
        first = s == 0 and not resumed
        high = jnp.max(scores, axis=1, keepdims=True) * SCALE
        high = jnp.broadcast_to(high, (SUB_ROWS, HEAD))
        if not first:
            high = jnp.maximum(top, high)
        weights = jnp.exp2(scores * SCALE - across(high, ROWS)).astype(jnp.bfloat16)
        widened = jnp.concatenate([columns(s, 1, h), ones], axis=1)
        product = jnp.dot(weights, widened, preferred_element_type=jnp.float32)
        if not first:
            product = product + total * across(jnp.exp2(top - high), 2 * HEAD)
        top, total = high, product
        if s == sources - 1:
            if final:
                row_sum = total[:, HEAD:]
                out_ref[at, mine] = (total[:, :HEAD] / row_sum).astype(out_ref.dtype)
                logs.append(top + jnp.log2(row_sum))
            else:
                out_ref[h, at, : 2 * HEAD] = total
                out_ref[h, at, 2 * HEAD :] = top
        scores = upcoming
        if final and s == sources - 1 and t == tiles - 1:
            eye = diagonal()
            lines = []
            for log in logs:
                for g in range(SUB_ROWS // HEAD):
                    piece = log[g * HEAD : (g + 1) * HEAD]
                    lines.append(jnp.sum(jnp.where(eye, piece, 0.0), axis=0, keepdims=True))
            lines.append(jnp.zeros((8 - len(lines), HEAD), jnp.float32))
            whole = jnp.concatenate(lines, axis=0)
            part1 = whole.astype(jnp.bfloat16)
            rest = whole - part1.astype(jnp.float32)
            part2 = rest.astype(jnp.bfloat16)
            part3 = (rest - part2.astype(jnp.float32)).astype(jnp.bfloat16)
            out_ref[ROWS:, mine] = jnp.concatenate(
                [part1, part2, part3, jnp.zeros((8, HEAD), jnp.bfloat16)], axis=0
            )
            logs = []


def attend(queries, sources, state=None, final=False):
    whole = pl.BlockSpec(memory_space=pltpu.VMEM)
    operands, places = [queries], []
    for source in sources:
        place = []
        for array, first in (source[:2], source[2:]):
            known = [i for i, operand in enumerate(operands) if operand is array and i > 0]
            if not known:
                operands.append(array)
            place.append((known[0] if known else len(operands) - 1, first))
        places.append(place)
    if state is not None:
        operands.append(state)
    if final:
        out_shape = jax.ShapeDtypeStruct((SENT_ROWS, WIDTH), jnp.bfloat16)
    else:
        out_shape = jax.ShapeDtypeStruct((HEADS_HERE, ROWS, 3 * HEAD), jnp.float32)
    return pl.pallas_call(
        functools.partial(
            attend_kernel,
            places=places,
            resumed=state is not None,
            final=final,
        ),
        in_specs=[whole] * len(operands),
        out_specs=whole,
        out_shape=out_shape,
        compiler_params=pltpu.CompilerParams(vmem_limit_bytes=VMEM),
        cost_estimate=pl.CostEstimate(flops=1, bytes_accessed=1, transcendentals=0),
    )(*operands)


def merge_kernel(*refs):
    *parts, out_ref = refs
    logs = []
    for part in parts:
        stats = part[ROWS:, :].astype(jnp.float32)
        logs.append(stats[0:8] + (stats[8:16] + stats[16:24]))
    high = functools.reduce(jnp.maximum, logs)
    shares = [jnp.exp2(log - high) for log in logs]
    whole = functools.reduce(jnp.add, shares)
    shares = [share / whole for share in shares]
    eye = diagonal()
    ones = jnp.ones((2 * HEAD, HEAD), jnp.bfloat16)
    for h in range(HEADS_HERE):
        mine = slice(h * HEAD, (h + 1) * HEAD)
        for g in range(ROWS // HEAD):
            at = slice(g * HEAD, (g + 1) * HEAD)
            total = None
            for part, share in zip(parts, shares):
                spread = jnp.where(eye, share[g : g + 1, mine], 0.0)
                coarse = spread.astype(jnp.bfloat16)
                fine = (spread - coarse.astype(jnp.float32)).astype(jnp.bfloat16)
                column = jnp.dot(
                    jnp.concatenate([coarse, fine], axis=1),
                    ones,
                    preferred_element_type=jnp.float32,
                )
                term = part[at, mine].astype(jnp.float32) * column
                total = term if total is None else total + term
            out_ref[at, mine] = total.astype(out_ref.dtype)


def merge(parts):
    return pl.pallas_call(
        merge_kernel,
        in_specs=[pl.BlockSpec(memory_space=pltpu.VMEM)] * len(parts),
        out_specs=pl.BlockSpec(memory_space=pltpu.VMEM),
        out_shape=jax.ShapeDtypeStruct((ROWS, WIDTH), jnp.bfloat16),
        compiler_params=pltpu.CompilerParams(vmem_limit_bytes=VMEM),
        cost_estimate=pl.CostEstimate(flops=1, bytes_accessed=1, transcendentals=0),
    )(*parts)


def swap(array, axis):
    pairs = {"c": [(0, 1)], "xl": [(0, 1)], "y01": [(0, 1), (2, 3)], "y12": [(1, 2), (3, 0)]}[axis]
    both = pairs + [(j, i) for i, j in pairs]
    return lax.ppermute(array, axis[0] if axis[0] == "y" else axis, both)


def after(first, *rest):
    return lax.optimization_barrier((first, *rest))


def per_device(queries, key_states, value_states):
    grouped = regroup(queries[0], key_states[0], value_states[0])
    own = lax.all_to_all(grouped, ULY, 0, 0).reshape(ROWS, 3 * WIDTH)
    own_q, own_kv = own[:, :WIDTH], own[:, WIDTH:]

    core_kv = swap(own_kv, "c")
    far_q = swap(own_q, "y12")
    side_kv = swap(own_kv, "xl")
    next_kv = swap(own_kv, "y01")

    def whole(array):
        return (array, 0, array, WIDTH)

    near = [(own, WIDTH, own, 2 * WIDTH), whole(core_kv)]
    state_own = attend(own, near)
    far_q, state_own = after(far_q, state_own)
    state_far = attend(far_q, near)
    side_kv, next_kv, state_far = after(side_kv, next_kv, state_far)
    side_core_kv = swap(side_kv, "c")
    next_core_kv = swap(next_kv, "c")
    diagonal_k = swap(next_kv[:, :WIDTH], "xl")
    diagonal_v = swap(side_kv[:, WIDTH:], "y01")

    side = [whole(side_kv), whole(side_core_kv)]
    beyond = [whole(next_kv), whole(next_core_kv)]
    state_own, state_far = after(attend(own, side, state_own), state_far)
    state_far = attend(far_q, side + beyond, state_far)
    state_far, diagonal_k, diagonal_v = after(state_far, diagonal_k, diagonal_v)
    diagonal_core_k = swap(diagonal_k, "c")
    diagonal_core_v = swap(diagonal_v, "c")
    diagonal = (diagonal_k, 0, diagonal_v, 0)
    diagonal_core = (diagonal_core_k, 0, diagonal_core_v, 0)
    state_far = attend(far_q, [diagonal], state_far)
    back = swap(attend(far_q, [diagonal_core], state_far, final=True), "y12")
    mine = attend(own, beyond + [diagonal, diagonal_core], state_own, final=True)

    merged = merge([mine, back]).reshape(GROUPS, TOKENS, WIDTH)
    return ungroup(lax.all_to_all(merged, ULY, 0, 0))[None]


def solution(mesh):
    split = Mesh(mesh.devices.reshape(4, 2, 2, 4, 2), ("z", "xh", "xl", "y", "c"))
    placed = P(None, ("z", "xh", "xl", "y", "c"), None)
    return jax.shard_map(
        per_device,
        mesh=split,
        in_specs=(placed, placed, placed),
        out_specs=placed,
        check_vma=False,
    )
```

```python
import functools
import math

import jax
import jax.numpy as jnp
from jax import lax
from jax.experimental import pallas as pl
from jax.experimental.pallas import tpu as pltpu
from jax.sharding import Mesh
from jax.sharding import PartitionSpec as P

HEAD = 128
HEADS_HERE = 3
WIDTH = HEAD * HEADS_HERE
GROUPS = 8
TOKENS = 96
ROWS = GROUPS * TOKENS
STAT_ROWS = 32
SENT_ROWS = ROWS + STAT_ROWS
SUB_ROWS = 256
SCALE = math.log2(math.e) / math.sqrt(HEAD)
ULY = ("z", "xh")
VMEM = 20 * 2**20


def regroup_kernel(*refs):
    count = (len(refs) - 2) // 2
    in_refs, out_ref, held, sems = refs[:count], refs[count], refs[count + 1 : -1], refs[-1]
    copies = [
        pltpu.make_async_copy(ref, block, sems.at[part])
        for part, (ref, block) in enumerate(zip(in_refs, held))
    ]
    for copy in copies:
        copy.start()
    for part, (copy, block) in enumerate(zip(copies, held)):
        copy.wait()
        for g in range(GROUPS):
            out_ref[g, :, part * WIDTH : (part + 1) * WIDTH] = block[:, g * WIDTH : (g + 1) * WIDTH]


def regroup(*arrays):
    return pl.pallas_call(
        regroup_kernel,
        in_specs=[pl.BlockSpec(memory_space=pl.ANY)] * len(arrays),
        out_specs=pl.BlockSpec(memory_space=pltpu.VMEM),
        out_shape=jax.ShapeDtypeStruct((GROUPS, TOKENS, len(arrays) * WIDTH), arrays[0].dtype),
        scratch_shapes=[pltpu.VMEM(array.shape, array.dtype) for array in arrays]
        + [pltpu.SemaphoreType.DMA((len(arrays),))],
        compiler_params=pltpu.CompilerParams(vmem_limit_bytes=VMEM),
    )(*arrays)


def copy_out_kernel(in_ref, out_ref, held, sem):
    copy = pltpu.make_async_copy(in_ref, held, sem)
    copy.start()
    copy.wait()
    for g in range(GROUPS):
        for x in range(2):
            out_ref[2 * g + x] = held[:, g * WIDTH : (g + 1) * WIDTH]


def copy_out(queries):
    return pl.pallas_call(
        copy_out_kernel,
        in_specs=[pl.BlockSpec(memory_space=pl.ANY)],
        out_specs=pl.BlockSpec(memory_space=pltpu.VMEM),
        out_shape=jax.ShapeDtypeStruct((2 * GROUPS, TOKENS, WIDTH), queries.dtype),
        scratch_shapes=[pltpu.VMEM(queries.shape, queries.dtype), pltpu.SemaphoreType.DMA],
        compiler_params=pltpu.CompilerParams(vmem_limit_bytes=VMEM),
    )(queries)


def part_kernel(in_ref, own_ref, far_ref):
    own = lax.axis_index("xl")
    for g in range(GROUPS):
        at = slice(g * TOKENS, (g + 1) * TOKENS)
        own_ref[at, :] = in_ref[2 * g + own]
        far_ref[at, :] = in_ref[2 * g + 1 - own]


def part(both):
    whole = pl.BlockSpec(memory_space=pltpu.VMEM)
    return pl.pallas_call(
        part_kernel,
        in_specs=[whole],
        out_specs=[whole, whole],
        out_shape=[jax.ShapeDtypeStruct((ROWS, WIDTH), both.dtype)] * 2,
        compiler_params=pltpu.CompilerParams(vmem_limit_bytes=VMEM),
        cost_estimate=pl.CostEstimate(flops=1, bytes_accessed=1, transcendentals=0),
    )(both)


def ungroup_kernel(in_ref, out_ref):
    for g in range(GROUPS):
        out_ref[:, g * WIDTH : (g + 1) * WIDTH] = in_ref[g]


def ungroup(parts):
    whole = pl.BlockSpec(memory_space=pltpu.VMEM)
    return pl.pallas_call(
        ungroup_kernel,
        in_specs=[whole],
        out_specs=whole,
        out_shape=jax.ShapeDtypeStruct((TOKENS, GROUPS * WIDTH), parts.dtype),
        compiler_params=pltpu.CompilerParams(vmem_limit_bytes=VMEM),
    )(parts)


def diagonal():
    rows = lax.broadcasted_iota(jnp.int32, (HEAD, HEAD), 0)
    cols = lax.broadcasted_iota(jnp.int32, (HEAD, HEAD), 1)
    return rows == cols


def across(column, width):
    return jnp.concatenate([column] * (width // HEAD), axis=1)


def attend_kernel(*refs, places, resumed, final):
    q_ref = refs[0]
    sources = len(places)
    state_ref = refs[-2] if resumed else None
    out_ref = refs[-1]
    tiles = ROWS // SUB_ROWS
    jobs = [(h, t, s) for h in range(HEADS_HERE) for t in range(tiles) for s in range(sources)]
    ones = jnp.ones((ROWS, HEAD), jnp.bfloat16)

    def columns(s, which, h):
        ref, first = places[s][which]
        at = first + h * HEAD
        return refs[ref][:, at : at + HEAD]

    def scores_of(h, t, s):
        return lax.dot_general(
            q_ref[t * SUB_ROWS : (t + 1) * SUB_ROWS, h * HEAD : (h + 1) * HEAD],
            columns(s, 0, h),
            (((1,), (1,)), ((), ())),
            preferred_element_type=jnp.float32,
        )

    top = total = None
    logs = []
    scores = scores_of(*jobs[0])
    for n, (h, t, s) in enumerate(jobs):
        upcoming = scores_of(*jobs[n + 1]) if n + 1 < len(jobs) else None
        at = slice(t * SUB_ROWS, (t + 1) * SUB_ROWS)
        mine = slice(h * HEAD, (h + 1) * HEAD)
        if s == 0 and resumed:
            total = state_ref[h, at, : 2 * HEAD]
            top = state_ref[h, at, 2 * HEAD :]
        first = s == 0 and not resumed
        high = jnp.max(scores, axis=1, keepdims=True) * SCALE
        high = jnp.broadcast_to(high, (SUB_ROWS, HEAD))
        if not first:
            high = jnp.maximum(top, high)
        weights = jnp.exp2(scores * SCALE - across(high, ROWS)).astype(jnp.bfloat16)
        widened = jnp.concatenate([columns(s, 1, h), ones], axis=1)
        product = jnp.dot(weights, widened, preferred_element_type=jnp.float32)
        if not first:
            product = product + total * across(jnp.exp2(top - high), 2 * HEAD)
        top, total = high, product
        if s == sources - 1:
            if final:
                row_sum = total[:, HEAD:]
                out_ref[at, mine] = (total[:, :HEAD] / row_sum).astype(out_ref.dtype)
                logs.append(top + jnp.log2(row_sum))
            else:
                out_ref[h, at, : 2 * HEAD] = total
                out_ref[h, at, 2 * HEAD :] = top
        scores = upcoming
        if final and s == sources - 1 and t == tiles - 1:
            eye = diagonal()
            lines = []
            for log in logs:
                for g in range(SUB_ROWS // HEAD):
                    piece = log[g * HEAD : (g + 1) * HEAD]
                    lines.append(jnp.sum(jnp.where(eye, piece, 0.0), axis=0, keepdims=True))
            lines.append(jnp.zeros((8 - len(lines), HEAD), jnp.float32))
            whole = jnp.concatenate(lines, axis=0)
            part1 = whole.astype(jnp.bfloat16)
            rest = whole - part1.astype(jnp.float32)
            part2 = rest.astype(jnp.bfloat16)
            part3 = (rest - part2.astype(jnp.float32)).astype(jnp.bfloat16)
            out_ref[ROWS:, mine] = jnp.concatenate(
                [part1, part2, part3, jnp.zeros((8, HEAD), jnp.bfloat16)], axis=0
            )
            logs = []


def attend(queries, sources, state=None, final=False):
    whole = pl.BlockSpec(memory_space=pltpu.VMEM)
    operands, places = [queries], []
    for source in sources:
        place = []
        for array, first in (source[:2], source[2:]):
            known = [i for i, operand in enumerate(operands) if operand is array and i > 0]
            if not known:
                operands.append(array)
            place.append((known[0] if known else len(operands) - 1, first))
        places.append(place)
    if state is not None:
        operands.append(state)
    if final:
        out_shape = jax.ShapeDtypeStruct((SENT_ROWS, WIDTH), jnp.bfloat16)
    else:
        out_shape = jax.ShapeDtypeStruct((HEADS_HERE, ROWS, 3 * HEAD), jnp.float32)
    return pl.pallas_call(
        functools.partial(
            attend_kernel,
            places=places,
            resumed=state is not None,
            final=final,
        ),
        in_specs=[whole] * len(operands),
        out_specs=whole,
        out_shape=out_shape,
        compiler_params=pltpu.CompilerParams(vmem_limit_bytes=VMEM),
        cost_estimate=pl.CostEstimate(flops=1, bytes_accessed=1, transcendentals=0),
    )(*operands)


def merge_kernel(*refs):
    *parts, out_ref = refs
    logs = []
    for part in parts:
        stats = part[ROWS:, :].astype(jnp.float32)
        logs.append(stats[0:8] + (stats[8:16] + stats[16:24]))
    high = functools.reduce(jnp.maximum, logs)
    shares = [jnp.exp2(log - high) for log in logs]
    whole = functools.reduce(jnp.add, shares)
    shares = [share / whole for share in shares]
    eye = diagonal()
    ones = jnp.ones((2 * HEAD, HEAD), jnp.bfloat16)
    for h in range(HEADS_HERE):
        mine = slice(h * HEAD, (h + 1) * HEAD)
        for g in range(ROWS // HEAD):
            at = slice(g * HEAD, (g + 1) * HEAD)
            total = None
            for part, share in zip(parts, shares):
                spread = jnp.where(eye, share[g : g + 1, mine], 0.0)
                coarse = spread.astype(jnp.bfloat16)
                fine = (spread - coarse.astype(jnp.float32)).astype(jnp.bfloat16)
                column = jnp.dot(
                    jnp.concatenate([coarse, fine], axis=1),
                    ones,
                    preferred_element_type=jnp.float32,
                )
                term = part[at, mine].astype(jnp.float32) * column
                total = term if total is None else total + term
            out_ref[at, mine] = total.astype(out_ref.dtype)


def merge(parts):
    return pl.pallas_call(
        merge_kernel,
        in_specs=[pl.BlockSpec(memory_space=pltpu.VMEM)] * len(parts),
        out_specs=pl.BlockSpec(memory_space=pltpu.VMEM),
        out_shape=jax.ShapeDtypeStruct((ROWS, WIDTH), jnp.bfloat16),
        compiler_params=pltpu.CompilerParams(vmem_limit_bytes=VMEM),
        cost_estimate=pl.CostEstimate(flops=1, bytes_accessed=1, transcendentals=0),
    )(*parts)


def swap(array, axis):
    pairs = {"c": [(0, 1)], "xl": [(0, 1)], "y01": [(0, 1), (2, 3)], "y12": [(1, 2), (3, 0)]}[axis]
    both = pairs + [(j, i) for i, j in pairs]
    return lax.ppermute(array, axis[0] if axis[0] == "y" else axis, both)


def after(first, *rest):
    return lax.optimization_barrier((first, *rest))


def per_device(queries, key_states, value_states):
    grouped_kv = regroup(key_states[0], value_states[0])
    own_kv = lax.all_to_all(grouped_kv, ULY, 0, 0).reshape(ROWS, 2 * WIDTH)
    own_kv, queries = after(own_kv, queries)
    next_kv = swap(own_kv, "y01")
    side_kv = swap(own_kv, "y12")
    core_kv = swap(own_kv, "c")
    both_q = lax.all_to_all(copy_out(queries[0]), ("z", "xh", "xl"), 0, 0)
    own_q, far_q = part(both_q)

    def whole(array):
        return (array, 0, array, WIDTH)

    near = [whole(own_kv), whole(core_kv)]
    state_far = attend(far_q, near)
    side_kv, next_kv, state_far = after(side_kv, next_kv, state_far)
    side_core_kv = swap(side_kv, "c")
    next_core_kv = swap(next_kv, "c")
    diagonal_k = swap(next_kv[:, :WIDTH], "y12")
    diagonal_v = swap(side_kv[:, WIDTH:], "y01")

    around = [whole(side_kv), whole(side_core_kv), whole(next_kv), whole(next_core_kv)]
    state_far = attend(far_q, around, state_far)
    state_far, own_q = after(state_far, own_q)
    state_own = attend(own_q, near)
    state_own, state_far, diagonal_k, diagonal_v = after(
        state_own, state_far, diagonal_k, diagonal_v
    )
    diagonal_core_k = swap(diagonal_k, "c")
    diagonal_core_v = swap(diagonal_v, "c")
    diagonal = (diagonal_k, 0, diagonal_v, 0)
    diagonal_core = (diagonal_core_k, 0, diagonal_core_v, 0)
    state_far = attend(far_q, [diagonal], state_far)
    back = swap(attend(far_q, [diagonal_core], state_far, final=True), "xl")
    mine = attend(own_q, around + [diagonal, diagonal_core], state_own, final=True)

    merged = merge([mine, back]).reshape(GROUPS, TOKENS, WIDTH)
    return ungroup(lax.all_to_all(merged, ULY, 0, 0))[None]


def solution(mesh):
    split = Mesh(mesh.devices.reshape(4, 2, 2, 4, 2), ("z", "xh", "xl", "y", "c"))
    placed = P(None, ("z", "xh", "xl", "y", "c"), None)
    return jax.shard_map(
        per_device,
        mesh=split,
        in_specs=(placed, placed, placed),
        out_specs=placed,
        check_vma=False,
    )
```

```python
import functools
import math

import jax
import jax.numpy as jnp
from jax import lax
from jax.experimental import pallas as pl
from jax.experimental.pallas import tpu as pltpu
from jax.sharding import Mesh
from jax.sharding import PartitionSpec as P

HEAD = 128
HEADS_HERE = 3
WIDTH = HEAD * HEADS_HERE
GROUPS = 8
TOKENS = 96
ROWS = GROUPS * TOKENS
STAT_ROWS = 32
SENT_ROWS = ROWS + STAT_ROWS
SUB_ROWS = 256
SCALE = math.log2(math.e) / math.sqrt(HEAD)
ULY = ("z", "xh")
VMEM = 20 * 2**20
WHOLE_VMEM = 60 * 2**20


def regroup_kernel(*refs):
    count = (len(refs) - 2) // 2
    in_refs, out_ref, held, sems = refs[:count], refs[count], refs[count + 1 : -1], refs[-1]
    copies = [
        pltpu.make_async_copy(ref, block, sems.at[part])
        for part, (ref, block) in enumerate(zip(in_refs, held))
    ]
    for copy in copies:
        copy.start()
    for part, (copy, block) in enumerate(zip(copies, held)):
        copy.wait()
        for g in range(GROUPS):
            out_ref[g, :, part * WIDTH : (part + 1) * WIDTH] = block[:, g * WIDTH : (g + 1) * WIDTH]


def regroup(*arrays):
    return pl.pallas_call(
        regroup_kernel,
        in_specs=[pl.BlockSpec(memory_space=pl.ANY)] * len(arrays),
        out_specs=pl.BlockSpec(memory_space=pltpu.VMEM),
        out_shape=jax.ShapeDtypeStruct((GROUPS, TOKENS, len(arrays) * WIDTH), arrays[0].dtype),
        scratch_shapes=[pltpu.VMEM(array.shape, array.dtype) for array in arrays]
        + [pltpu.SemaphoreType.DMA((len(arrays),))],
        compiler_params=pltpu.CompilerParams(vmem_limit_bytes=WHOLE_VMEM),
    )(*arrays)


def copy_out_kernel(in_ref, out_ref, held, sem):
    copy = pltpu.make_async_copy(in_ref, held, sem)
    copy.start()
    copy.wait()
    for g in range(GROUPS):
        for x in range(2):
            out_ref[2 * g + x] = held[:, g * WIDTH : (g + 1) * WIDTH]


def copy_out(queries):
    return pl.pallas_call(
        copy_out_kernel,
        in_specs=[pl.BlockSpec(memory_space=pl.ANY)],
        out_specs=pl.BlockSpec(memory_space=pltpu.VMEM),
        out_shape=jax.ShapeDtypeStruct((2 * GROUPS, TOKENS, WIDTH), queries.dtype),
        scratch_shapes=[pltpu.VMEM(queries.shape, queries.dtype), pltpu.SemaphoreType.DMA],
        compiler_params=pltpu.CompilerParams(vmem_limit_bytes=VMEM),
    )(queries)


def part_kernel(in_ref, own_ref, far_ref):
    own = lax.axis_index("xl")
    for g in range(GROUPS):
        at = slice(g * TOKENS, (g + 1) * TOKENS)
        own_ref[at, :] = in_ref[2 * g + own]
        far_ref[at, :] = in_ref[2 * g + 1 - own]


def part(both):
    whole = pl.BlockSpec(memory_space=pltpu.VMEM)
    return pl.pallas_call(
        part_kernel,
        in_specs=[whole],
        out_specs=[whole, whole],
        out_shape=[jax.ShapeDtypeStruct((ROWS, WIDTH), both.dtype)] * 2,
        compiler_params=pltpu.CompilerParams(vmem_limit_bytes=VMEM),
        cost_estimate=pl.CostEstimate(flops=1, bytes_accessed=1, transcendentals=0),
    )(both)


def ungroup_kernel(in_ref, out_ref):
    for g in range(GROUPS):
        out_ref[:, g * WIDTH : (g + 1) * WIDTH] = in_ref[g]


def ungroup(parts):
    whole = pl.BlockSpec(memory_space=pltpu.VMEM)
    return pl.pallas_call(
        ungroup_kernel,
        in_specs=[whole],
        out_specs=whole,
        out_shape=jax.ShapeDtypeStruct((TOKENS, GROUPS * WIDTH), parts.dtype),
        compiler_params=pltpu.CompilerParams(vmem_limit_bytes=VMEM),
    )(parts)


def diagonal():
    rows = lax.broadcasted_iota(jnp.int32, (HEAD, HEAD), 0)
    cols = lax.broadcasted_iota(jnp.int32, (HEAD, HEAD), 1)
    return rows == cols


def across(column, width):
    return jnp.concatenate([column] * (width // HEAD), axis=1)


def attend_kernel(*refs, places, resumed, final):
    q_ref = refs[0]
    sources = len(places)
    state_ref = refs[-2] if resumed else None
    out_ref = refs[-1]
    tiles = ROWS // SUB_ROWS
    jobs = [(h, t, s) for h in range(HEADS_HERE) for t in range(tiles) for s in range(sources)]
    ones = jnp.ones((ROWS, HEAD), jnp.bfloat16)

    def columns(s, which, h):
        ref, first = places[s][which]
        at = first + h * HEAD
        return refs[ref][:, at : at + HEAD]

    def scores_of(h, t, s):
        return lax.dot_general(
            q_ref[t * SUB_ROWS : (t + 1) * SUB_ROWS, h * HEAD : (h + 1) * HEAD],
            columns(s, 0, h),
            (((1,), (1,)), ((), ())),
            preferred_element_type=jnp.float32,
        )

    top = total = None
    logs = []
    scores = scores_of(*jobs[0])
    for n, (h, t, s) in enumerate(jobs):
        upcoming = scores_of(*jobs[n + 1]) if n + 1 < len(jobs) else None
        at = slice(t * SUB_ROWS, (t + 1) * SUB_ROWS)
        mine = slice(h * HEAD, (h + 1) * HEAD)
        if s == 0 and resumed:
            total = state_ref[h, at, : 2 * HEAD]
            top = state_ref[h, at, 2 * HEAD :]
        first = s == 0 and not resumed
        high = jnp.max(scores, axis=1, keepdims=True) * SCALE
        high = jnp.broadcast_to(high, (SUB_ROWS, HEAD))
        if not first:
            high = jnp.maximum(top, high)
        weights = jnp.exp2(scores * SCALE - across(high, ROWS)).astype(jnp.bfloat16)
        widened = jnp.concatenate([columns(s, 1, h), ones], axis=1)
        product = jnp.dot(weights, widened, preferred_element_type=jnp.float32)
        if not first:
            product = product + total * across(jnp.exp2(top - high), 2 * HEAD)
        top, total = high, product
        if s == sources - 1:
            if final:
                row_sum = total[:, HEAD:]
                out_ref[at, mine] = (total[:, :HEAD] / row_sum).astype(out_ref.dtype)
                logs.append(top + jnp.log2(row_sum))
            else:
                out_ref[h, at, : 2 * HEAD] = total
                out_ref[h, at, 2 * HEAD :] = top
        scores = upcoming
        if final and s == sources - 1 and t == tiles - 1:
            eye = diagonal()
            lines = []
            for log in logs:
                for g in range(SUB_ROWS // HEAD):
                    piece = log[g * HEAD : (g + 1) * HEAD]
                    lines.append(jnp.sum(jnp.where(eye, piece, 0.0), axis=0, keepdims=True))
            lines.append(jnp.zeros((8 - len(lines), HEAD), jnp.float32))
            whole = jnp.concatenate(lines, axis=0)
            part1 = whole.astype(jnp.bfloat16)
            rest = whole - part1.astype(jnp.float32)
            part2 = rest.astype(jnp.bfloat16)
            part3 = (rest - part2.astype(jnp.float32)).astype(jnp.bfloat16)
            out_ref[ROWS:, mine] = jnp.concatenate(
                [part1, part2, part3, jnp.zeros((8, HEAD), jnp.bfloat16)], axis=0
            )
            logs = []


def attend(queries, sources, state=None, final=False):
    whole = pl.BlockSpec(memory_space=pltpu.VMEM)
    operands, places = [queries], []
    for source in sources:
        place = []
        for array, first in (source[:2], source[2:]):
            known = [i for i, operand in enumerate(operands) if operand is array and i > 0]
            if not known:
                operands.append(array)
            place.append((known[0] if known else len(operands) - 1, first))
        places.append(place)
    if state is not None:
        operands.append(state)
    if final:
        out_shape = jax.ShapeDtypeStruct((SENT_ROWS, WIDTH), jnp.bfloat16)
    else:
        out_shape = jax.ShapeDtypeStruct((HEADS_HERE, ROWS, 3 * HEAD), jnp.float32)
    return pl.pallas_call(
        functools.partial(
            attend_kernel,
            places=places,
            resumed=state is not None,
            final=final,
        ),
        in_specs=[whole] * len(operands),
        out_specs=whole,
        out_shape=out_shape,
        compiler_params=pltpu.CompilerParams(vmem_limit_bytes=VMEM),
        cost_estimate=pl.CostEstimate(flops=1, bytes_accessed=1, transcendentals=0),
    )(*operands)


def merge_kernel(*refs):
    *parts, out_ref = refs
    logs = []
    for part in parts:
        stats = part[ROWS:, :].astype(jnp.float32)
        logs.append(stats[0:8] + (stats[8:16] + stats[16:24]))
    high = functools.reduce(jnp.maximum, logs)
    shares = [jnp.exp2(log - high) for log in logs]
    whole = functools.reduce(jnp.add, shares)
    shares = [share / whole for share in shares]
    eye = diagonal()
    ones = jnp.ones((2 * HEAD, HEAD), jnp.bfloat16)
    for h in range(HEADS_HERE):
        mine = slice(h * HEAD, (h + 1) * HEAD)
        for g in range(ROWS // HEAD):
            at = slice(g * HEAD, (g + 1) * HEAD)
            total = None
            for part, share in zip(parts, shares):
                spread = jnp.where(eye, share[g : g + 1, mine], 0.0)
                coarse = spread.astype(jnp.bfloat16)
                fine = (spread - coarse.astype(jnp.float32)).astype(jnp.bfloat16)
                column = jnp.dot(
                    jnp.concatenate([coarse, fine], axis=1),
                    ones,
                    preferred_element_type=jnp.float32,
                )
                term = part[at, mine].astype(jnp.float32) * column
                total = term if total is None else total + term
            out_ref[at, mine] = total.astype(out_ref.dtype)


def merge(parts):
    return pl.pallas_call(
        merge_kernel,
        in_specs=[pl.BlockSpec(memory_space=pltpu.VMEM)] * len(parts),
        out_specs=pl.BlockSpec(memory_space=pltpu.VMEM),
        out_shape=jax.ShapeDtypeStruct((ROWS, WIDTH), jnp.bfloat16),
        compiler_params=pltpu.CompilerParams(vmem_limit_bytes=VMEM),
        cost_estimate=pl.CostEstimate(flops=1, bytes_accessed=1, transcendentals=0),
    )(*parts)


def swap(array, axis):
    pairs = {"c": [(0, 1)], "xl": [(0, 1)], "y01": [(0, 1), (2, 3)], "y12": [(1, 2), (3, 0)]}[axis]
    both = pairs + [(j, i) for i, j in pairs]
    return lax.ppermute(array, axis[0] if axis[0] == "y" else axis, both)


def after(first, *rest):
    return lax.optimization_barrier((first, *rest))


def per_device(queries, key_states, value_states):
    grouped_kv = regroup(key_states[0], value_states[0])
    own_kv = lax.all_to_all(grouped_kv, ULY, 0, 0).reshape(ROWS, 2 * WIDTH)
    own_kv, queries = after(own_kv, queries)
    next_kv = swap(own_kv, "y01")
    side_kv = swap(own_kv, "y12")
    core_kv = swap(own_kv, "c")
    both_q = lax.all_to_all(copy_out(queries[0]), ("z", "xh", "xl"), 0, 0)
    own_q, far_q = part(both_q)

    def whole(array):
        return (array, 0, array, WIDTH)

    near = [whole(own_kv), whole(core_kv)]
    state_far = attend(far_q, near)
    side_kv, next_kv, state_far = after(side_kv, next_kv, state_far)
    side_core_kv = swap(side_kv, "c")
    next_core_kv = swap(next_kv, "c")
    diagonal_k = swap(next_kv[:, :WIDTH], "y12")
    diagonal_v = swap(side_kv[:, WIDTH:], "y01")

    around = [whole(side_kv), whole(side_core_kv), whole(next_kv), whole(next_core_kv)]
    own_q, state_far = after(own_q, state_far)
    state_own = attend(own_q, near)
    state_far, state_own = after(state_far, state_own)
    state_far = attend(far_q, around, state_far)
    state_far, diagonal_k, diagonal_v = after(state_far, diagonal_k, diagonal_v)
    diagonal_core_k = swap(diagonal_k, "c")
    diagonal_core_v = swap(diagonal_v, "c")
    diagonal = (diagonal_k, 0, diagonal_v, 0)
    diagonal_core = (diagonal_core_k, 0, diagonal_core_v, 0)
    state_far = attend(far_q, [diagonal], state_far)
    back = swap(attend(far_q, [diagonal_core], state_far, final=True), "xl")
    mine = attend(own_q, around + [diagonal, diagonal_core], state_own, final=True)

    merged = merge([mine, back]).reshape(GROUPS, TOKENS, WIDTH)
    return ungroup(lax.all_to_all(merged, ULY, 0, 0))[None]


def solution(mesh):
    split = Mesh(mesh.devices.reshape(4, 2, 2, 4, 2), ("z", "xh", "xl", "y", "c"))
    placed = P(None, ("z", "xh", "xl", "y", "c"), None)
    return jax.shard_map(
        per_device,
        mesh=split,
        in_specs=(placed, placed, placed),
        out_specs=placed,
        check_vma=False,
    )
```

```python
import functools
import math

import jax
import jax.numpy as jnp
from jax import lax
from jax.experimental import pallas as pl
from jax.experimental.pallas import tpu as pltpu
from jax.sharding import Mesh
from jax.sharding import PartitionSpec as P

HEAD = 128
HEADS_HERE = 3
WIDTH = HEAD * HEADS_HERE
GROUPS = 8
TOKENS = 96
ROWS = GROUPS * TOKENS
STAT_ROWS = 32
SENT_ROWS = ROWS + STAT_ROWS
SUB_ROWS = 256
SCALE = math.log2(math.e) / math.sqrt(HEAD)
ULY = ("z", "xh")
VMEM = 20 * 2**20
WHOLE_VMEM = 60 * 2**20


def regroup_kernel(*refs):
    count = (len(refs) - 2) // 2
    in_refs, out_ref, held, sems = refs[:count], refs[count], refs[count + 1 : -1], refs[-1]
    copies = [
        pltpu.make_async_copy(ref, block, sems.at[part])
        for part, (ref, block) in enumerate(zip(in_refs, held))
    ]
    for copy in copies:
        copy.start()
    for part, (copy, block) in enumerate(zip(copies, held)):
        copy.wait()
        for g in range(GROUPS):
            out_ref[g, :, part * WIDTH : (part + 1) * WIDTH] = block[:, g * WIDTH : (g + 1) * WIDTH]


def regroup(*arrays):
    return pl.pallas_call(
        regroup_kernel,
        in_specs=[pl.BlockSpec(memory_space=pl.ANY)] * len(arrays),
        out_specs=pl.BlockSpec(memory_space=pltpu.VMEM),
        out_shape=jax.ShapeDtypeStruct((GROUPS, TOKENS, len(arrays) * WIDTH), arrays[0].dtype),
        scratch_shapes=[pltpu.VMEM(array.shape, array.dtype) for array in arrays]
        + [pltpu.SemaphoreType.DMA((len(arrays),))],
        compiler_params=pltpu.CompilerParams(vmem_limit_bytes=WHOLE_VMEM),
    )(*arrays)


def copy_out_kernel(in_ref, out_ref, held, sem):
    copy = pltpu.make_async_copy(in_ref, held, sem)
    copy.start()
    copy.wait()
    for g in range(GROUPS):
        for x in range(2):
            out_ref[2 * g + x] = held[:, g * WIDTH : (g + 1) * WIDTH]


def copy_out(queries):
    return pl.pallas_call(
        copy_out_kernel,
        in_specs=[pl.BlockSpec(memory_space=pl.ANY)],
        out_specs=pl.BlockSpec(memory_space=pltpu.VMEM),
        out_shape=jax.ShapeDtypeStruct((2 * GROUPS, TOKENS, WIDTH), queries.dtype),
        scratch_shapes=[pltpu.VMEM(queries.shape, queries.dtype), pltpu.SemaphoreType.DMA],
        compiler_params=pltpu.CompilerParams(vmem_limit_bytes=VMEM),
    )(queries)


def part_kernel(in_ref, own_ref, far_ref):
    own = lax.axis_index("xl")
    for g in range(GROUPS):
        at = slice(g * TOKENS, (g + 1) * TOKENS)
        own_ref[at, :] = in_ref[2 * g + own]
        far_ref[at, :] = in_ref[2 * g + 1 - own]


def part(both):
    whole = pl.BlockSpec(memory_space=pltpu.VMEM)
    return pl.pallas_call(
        part_kernel,
        in_specs=[whole],
        out_specs=[whole, whole],
        out_shape=[jax.ShapeDtypeStruct((ROWS, WIDTH), both.dtype)] * 2,
        compiler_params=pltpu.CompilerParams(vmem_limit_bytes=VMEM),
        cost_estimate=pl.CostEstimate(flops=1, bytes_accessed=1, transcendentals=0),
    )(both)


def ungroup_kernel(in_ref, out_ref):
    for g in range(GROUPS):
        out_ref[:, g * WIDTH : (g + 1) * WIDTH] = in_ref[g]


def ungroup(parts):
    whole = pl.BlockSpec(memory_space=pltpu.VMEM)
    return pl.pallas_call(
        ungroup_kernel,
        in_specs=[whole],
        out_specs=whole,
        out_shape=jax.ShapeDtypeStruct((TOKENS, GROUPS * WIDTH), parts.dtype),
        compiler_params=pltpu.CompilerParams(vmem_limit_bytes=VMEM),
    )(parts)


def diagonal():
    rows = lax.broadcasted_iota(jnp.int32, (HEAD, HEAD), 0)
    cols = lax.broadcasted_iota(jnp.int32, (HEAD, HEAD), 1)
    return rows == cols


def across(column, width):
    return jnp.concatenate([column] * (width // HEAD), axis=1)


def attend_kernel(*refs, heads, places, resumed, final):
    q_ref = refs[0]
    sources = len(places)
    state_ref = refs[-2] if resumed else None
    out_ref = refs[-1]
    tiles = ROWS // SUB_ROWS
    jobs = [(h, t, s) for h in heads for t in range(tiles) for s in range(sources)]
    ones = jnp.ones((ROWS, HEAD), jnp.bfloat16)

    def columns(s, which, h):
        ref, first = places[s][which]
        at = first + h * HEAD
        return refs[ref][:, at : at + HEAD]

    def scores_of(h, t, s):
        return lax.dot_general(
            q_ref[t * SUB_ROWS : (t + 1) * SUB_ROWS, h * HEAD : (h + 1) * HEAD],
            columns(s, 0, h),
            (((1,), (1,)), ((), ())),
            preferred_element_type=jnp.float32,
        )

    top = total = None
    logs = []
    scores = scores_of(*jobs[0])
    for n, (h, t, s) in enumerate(jobs):
        upcoming = scores_of(*jobs[n + 1]) if n + 1 < len(jobs) else None
        at = slice(t * SUB_ROWS, (t + 1) * SUB_ROWS)
        place = h - heads[0]
        mine = slice(place * HEAD, (place + 1) * HEAD)
        if s == 0 and resumed:
            total = state_ref[h, at, : 2 * HEAD]
            top = state_ref[h, at, 2 * HEAD :]
        first = s == 0 and not resumed
        high = jnp.max(scores, axis=1, keepdims=True) * SCALE
        high = jnp.broadcast_to(high, (SUB_ROWS, HEAD))
        if not first:
            high = jnp.maximum(top, high)
        weights = jnp.exp2(scores * SCALE - across(high, ROWS)).astype(jnp.bfloat16)
        widened = jnp.concatenate([columns(s, 1, h), ones], axis=1)
        product = jnp.dot(weights, widened, preferred_element_type=jnp.float32)
        if not first:
            product = product + total * across(jnp.exp2(top - high), 2 * HEAD)
        top, total = high, product
        if s == sources - 1:
            if final:
                row_sum = total[:, HEAD:]
                out_ref[at, mine] = (total[:, :HEAD] / row_sum).astype(out_ref.dtype)
                logs.append(top + jnp.log2(row_sum))
            else:
                out_ref[place, at, : 2 * HEAD] = total
                out_ref[place, at, 2 * HEAD :] = top
        scores = upcoming
        if final and s == sources - 1 and t == tiles - 1:
            eye = diagonal()
            lines = []
            for log in logs:
                for g in range(SUB_ROWS // HEAD):
                    piece = log[g * HEAD : (g + 1) * HEAD]
                    lines.append(jnp.sum(jnp.where(eye, piece, 0.0), axis=0, keepdims=True))
            lines.append(jnp.zeros((8 - len(lines), HEAD), jnp.float32))
            whole = jnp.concatenate(lines, axis=0)
            part1 = whole.astype(jnp.bfloat16)
            rest = whole - part1.astype(jnp.float32)
            part2 = rest.astype(jnp.bfloat16)
            part3 = (rest - part2.astype(jnp.float32)).astype(jnp.bfloat16)
            out_ref[ROWS:, mine] = jnp.concatenate(
                [part1, part2, part3, jnp.zeros((8, HEAD), jnp.bfloat16)], axis=0
            )
            logs = []


def attend(queries, sources, state=None, final=False, heads=(0, 1, 2), cost=1):
    whole = pl.BlockSpec(memory_space=pltpu.VMEM)
    operands, places = [queries], []
    for source in sources:
        place = []
        for array, first in (source[:2], source[2:]):
            known = [i for i, operand in enumerate(operands) if operand is array and i > 0]
            if not known:
                operands.append(array)
            place.append((known[0] if known else len(operands) - 1, first))
        places.append(place)
    if state is not None:
        operands.append(state)
    if final:
        out_shape = jax.ShapeDtypeStruct((SENT_ROWS, len(heads) * HEAD), jnp.bfloat16)
    else:
        out_shape = jax.ShapeDtypeStruct((len(heads), ROWS, 3 * HEAD), jnp.float32)
    return pl.pallas_call(
        functools.partial(
            attend_kernel,
            heads=heads,
            places=places,
            resumed=state is not None,
            final=final,
        ),
        in_specs=[whole] * len(operands),
        out_specs=whole,
        out_shape=out_shape,
        compiler_params=pltpu.CompilerParams(vmem_limit_bytes=VMEM),
        cost_estimate=pl.CostEstimate(flops=cost, bytes_accessed=1, transcendentals=0),
    )(*operands)


def merge_kernel(mine_ref, few_ref, many_ref, out_ref):
    eye = diagonal()
    ones = jnp.ones((2 * HEAD, HEAD), jnp.bfloat16)
    for h in range(HEADS_HERE):
        back_ref, place = (few_ref, 0) if h == 0 else (many_ref, h - 1)
        parts = [
            (mine_ref, slice(h * HEAD, (h + 1) * HEAD)),
            (back_ref, slice(place * HEAD, (place + 1) * HEAD)),
        ]
        logs = []
        for part, at in parts:
            stats = part[ROWS:, at].astype(jnp.float32)
            logs.append(stats[0:8] + (stats[8:16] + stats[16:24]))
        high = functools.reduce(jnp.maximum, logs)
        shares = [jnp.exp2(log - high) for log in logs]
        whole = functools.reduce(jnp.add, shares)
        shares = [share / whole for share in shares]
        for g in range(ROWS // HEAD):
            rows = slice(g * HEAD, (g + 1) * HEAD)
            total = None
            for (part, at), share in zip(parts, shares):
                spread = jnp.where(eye, share[g : g + 1, :], 0.0)
                coarse = spread.astype(jnp.bfloat16)
                fine = (spread - coarse.astype(jnp.float32)).astype(jnp.bfloat16)
                column = jnp.dot(
                    jnp.concatenate([coarse, fine], axis=1),
                    ones,
                    preferred_element_type=jnp.float32,
                )
                term = part[rows, at].astype(jnp.float32) * column
                total = term if total is None else total + term
            out_ref[rows, h * HEAD : (h + 1) * HEAD] = total.astype(out_ref.dtype)


def merge(parts):
    return pl.pallas_call(
        merge_kernel,
        in_specs=[pl.BlockSpec(memory_space=pltpu.VMEM)] * len(parts),
        out_specs=pl.BlockSpec(memory_space=pltpu.VMEM),
        out_shape=jax.ShapeDtypeStruct((ROWS, WIDTH), jnp.bfloat16),
        compiler_params=pltpu.CompilerParams(vmem_limit_bytes=VMEM),
        cost_estimate=pl.CostEstimate(flops=1, bytes_accessed=1, transcendentals=0),
    )(*parts)


def swap(array, axis):
    pairs = {"c": [(0, 1)], "xl": [(0, 1)], "y01": [(0, 1), (2, 3)], "y12": [(1, 2), (3, 0)]}[axis]
    both = pairs + [(j, i) for i, j in pairs]
    return lax.ppermute(array, axis[0] if axis[0] == "y" else axis, both)


def after(first, *rest):
    return lax.optimization_barrier((first, *rest))


def per_device(queries, key_states, value_states):
    grouped_kv = regroup(key_states[0], value_states[0])
    own_kv = lax.all_to_all(grouped_kv, ULY, 0, 0).reshape(ROWS, 2 * WIDTH)
    own_kv, queries = after(own_kv, queries)
    next_kv = swap(own_kv, "y01")
    side_kv = swap(own_kv, "y12")
    core_kv = swap(own_kv, "c")
    both_q = lax.all_to_all(copy_out(queries[0]), ("z", "xh", "xl"), 0, 0)
    own_q, far_q = part(both_q)

    def whole(array):
        return (array, 0, array, WIDTH)

    near = [whole(own_kv), whole(core_kv)]
    state_far = attend(far_q, near)
    side_kv, next_kv, state_far = after(side_kv, next_kv, state_far)
    side_core_kv = swap(side_kv, "c")
    next_core_kv = swap(next_kv, "c")
    diagonal_k = swap(next_kv[:, :WIDTH], "y12")
    diagonal_v = swap(side_kv[:, WIDTH:], "y01")

    around = [whole(side_kv), whole(side_core_kv), whole(next_kv), whole(next_core_kv)]
    own_q, state_far = after(own_q, state_far)
    state_own = attend(own_q, near)
    state_far, state_own = after(state_far, state_own)
    state_far = attend(far_q, around, state_far)
    state_far, diagonal_k, diagonal_v = after(state_far, diagonal_k, diagonal_v)
    diagonal_core_k = swap(diagonal_k, "c")
    diagonal_core_v = swap(diagonal_v, "c")
    diagonal = (diagonal_k, 0, diagonal_v, 0)
    diagonal_core = (diagonal_core_k, 0, diagonal_core_v, 0)
    state_far = attend(far_q, [diagonal], state_far)
    few = attend(far_q, [diagonal_core], state_far, final=True, heads=(0,))
    few, state_far = after(few, state_far)
    back_few = swap(few, "xl")
    many = attend(
        far_q, [diagonal_core], state_far, final=True, heads=(1, 2), cost=10**11
    )
    back_many = swap(many, "xl")
    mine = attend(own_q, around + [diagonal, diagonal_core], state_own, final=True)

    merged = merge([mine, back_few, back_many]).reshape(GROUPS, TOKENS, WIDTH)
    return ungroup(lax.all_to_all(merged, ULY, 0, 0))[None]


def solution(mesh):
    split = Mesh(mesh.devices.reshape(4, 2, 2, 4, 2), ("z", "xh", "xl", "y", "c"))
    placed = P(None, ("z", "xh", "xl", "y", "c"), None)
    return jax.shard_map(
        per_device,
        mesh=split,
        in_specs=(placed, placed, placed),
        out_specs=placed,
        check_vma=False,
    )
```

```python
import functools
import math

import jax
import jax.numpy as jnp
from jax import lax
from jax.experimental import pallas as pl
from jax.experimental.pallas import tpu as pltpu
from jax.sharding import Mesh
from jax.sharding import PartitionSpec as P

HEAD = 128
HEADS_HERE = 3
WIDTH = HEAD * HEADS_HERE
GROUPS = 8
TOKENS = 96
ROWS = GROUPS * TOKENS
STAT_ROWS = 32
SENT_ROWS = ROWS + STAT_ROWS
SUB_ROWS = 256
SCALE = math.log2(math.e) / math.sqrt(HEAD)
ULY = ("z", "xh")
VMEM = 20 * 2**20
WHOLE_VMEM = 60 * 2**20


def regroup_kernel(*refs):
    count = (len(refs) - 2) // 2
    in_refs, out_ref, held, sems = refs[:count], refs[count], refs[count + 1 : -1], refs[-1]
    copies = [
        pltpu.make_async_copy(ref, block, sems.at[part])
        for part, (ref, block) in enumerate(zip(in_refs, held))
    ]
    for copy in copies:
        copy.start()
    for part, (copy, block) in enumerate(zip(copies, held)):
        copy.wait()
        for g in range(GROUPS):
            out_ref[g, :, part * WIDTH : (part + 1) * WIDTH] = block[:, g * WIDTH : (g + 1) * WIDTH]


def regroup(*arrays):
    return pl.pallas_call(
        regroup_kernel,
        in_specs=[pl.BlockSpec(memory_space=pl.ANY)] * len(arrays),
        out_specs=pl.BlockSpec(memory_space=pltpu.VMEM),
        out_shape=jax.ShapeDtypeStruct((GROUPS, TOKENS, len(arrays) * WIDTH), arrays[0].dtype),
        scratch_shapes=[pltpu.VMEM(array.shape, array.dtype) for array in arrays]
        + [pltpu.SemaphoreType.DMA((len(arrays),))],
        compiler_params=pltpu.CompilerParams(vmem_limit_bytes=WHOLE_VMEM),
    )(*arrays)


def copy_out_kernel(in_ref, out_ref, held, sem):
    copy = pltpu.make_async_copy(in_ref, held, sem)
    copy.start()
    copy.wait()
    for g in range(GROUPS):
        for x in range(2):
            out_ref[2 * g + x] = held[:, g * WIDTH : (g + 1) * WIDTH]


def copy_out(queries):
    return pl.pallas_call(
        copy_out_kernel,
        in_specs=[pl.BlockSpec(memory_space=pl.ANY)],
        out_specs=pl.BlockSpec(memory_space=pltpu.VMEM),
        out_shape=jax.ShapeDtypeStruct((2 * GROUPS, TOKENS, WIDTH), queries.dtype),
        scratch_shapes=[pltpu.VMEM(queries.shape, queries.dtype), pltpu.SemaphoreType.DMA],
        compiler_params=pltpu.CompilerParams(vmem_limit_bytes=VMEM),
    )(queries)


def part_kernel(in_ref, own_ref, far_ref):
    own = lax.axis_index("xl")
    for g in range(GROUPS):
        at = slice(g * TOKENS, (g + 1) * TOKENS)
        own_ref[at, :] = in_ref[2 * g + own]
        far_ref[at, :] = in_ref[2 * g + 1 - own]


def part(both):
    whole = pl.BlockSpec(memory_space=pltpu.VMEM)
    return pl.pallas_call(
        part_kernel,
        in_specs=[whole],
        out_specs=[whole, whole],
        out_shape=[jax.ShapeDtypeStruct((ROWS, WIDTH), both.dtype)] * 2,
        compiler_params=pltpu.CompilerParams(vmem_limit_bytes=VMEM),
        cost_estimate=pl.CostEstimate(flops=1, bytes_accessed=1, transcendentals=0),
    )(both)


def ungroup_kernel(in_ref, out_ref):
    for g in range(GROUPS):
        out_ref[:, g * WIDTH : (g + 1) * WIDTH] = in_ref[g]


def ungroup(parts):
    whole = pl.BlockSpec(memory_space=pltpu.VMEM)
    return pl.pallas_call(
        ungroup_kernel,
        in_specs=[whole],
        out_specs=whole,
        out_shape=jax.ShapeDtypeStruct((TOKENS, GROUPS * WIDTH), parts.dtype),
        compiler_params=pltpu.CompilerParams(vmem_limit_bytes=VMEM),
    )(parts)


def diagonal():
    rows = lax.broadcasted_iota(jnp.int32, (HEAD, HEAD), 0)
    cols = lax.broadcasted_iota(jnp.int32, (HEAD, HEAD), 1)
    return rows == cols


def across(column, width):
    return jnp.concatenate([column] * (width // HEAD), axis=1)


def attend_kernel(*refs, heads, places, resumed, final):
    q_ref = refs[0]
    sources = len(places)
    state_ref = refs[-2] if resumed else None
    out_ref = refs[-1]
    tiles = ROWS // SUB_ROWS
    jobs = [(h, t, s) for h in heads for t in range(tiles) for s in range(sources)]
    ones = jnp.ones((ROWS, HEAD), jnp.bfloat16)

    def columns(s, which, h):
        ref, first = places[s][which]
        at = first + h * HEAD
        return refs[ref][:, at : at + HEAD]

    def scores_of(h, t, s):
        return lax.dot_general(
            q_ref[t * SUB_ROWS : (t + 1) * SUB_ROWS, h * HEAD : (h + 1) * HEAD],
            columns(s, 0, h),
            (((1,), (1,)), ((), ())),
            preferred_element_type=jnp.float32,
        )

    top = total = None
    logs = []
    scores = scores_of(*jobs[0])
    for n, (h, t, s) in enumerate(jobs):
        upcoming = scores_of(*jobs[n + 1]) if n + 1 < len(jobs) else None
        at = slice(t * SUB_ROWS, (t + 1) * SUB_ROWS)
        place = h - heads[0]
        mine = slice(place * HEAD, (place + 1) * HEAD)
        if s == 0 and resumed:
            total = state_ref[h, at, : 2 * HEAD]
            top = state_ref[h, at, 2 * HEAD :]
        first = s == 0 and not resumed
        high = jnp.max(scores, axis=1, keepdims=True) * SCALE
        high = jnp.broadcast_to(high, (SUB_ROWS, HEAD))
        if not first:
            high = jnp.maximum(top, high)
        weights = jnp.exp2(scores * SCALE - across(high, ROWS)).astype(jnp.bfloat16)
        widened = jnp.concatenate([columns(s, 1, h), ones], axis=1)
        product = jnp.dot(weights, widened, preferred_element_type=jnp.float32)
        if not first:
            product = product + total * across(jnp.exp2(top - high), 2 * HEAD)
        top, total = high, product
        if s == sources - 1:
            if final:
                row_sum = total[:, HEAD:]
                out_ref[at, mine] = (total[:, :HEAD] / row_sum).astype(out_ref.dtype)
                logs.append(top + jnp.log2(row_sum))
            else:
                out_ref[place, at, : 2 * HEAD] = total
                out_ref[place, at, 2 * HEAD :] = top
        scores = upcoming
        if final and s == sources - 1 and t == tiles - 1:
            eye = diagonal()
            lines = []
            for log in logs:
                for g in range(SUB_ROWS // HEAD):
                    piece = log[g * HEAD : (g + 1) * HEAD]
                    lines.append(jnp.sum(jnp.where(eye, piece, 0.0), axis=0, keepdims=True))
            lines.append(jnp.zeros((8 - len(lines), HEAD), jnp.float32))
            whole = jnp.concatenate(lines, axis=0)
            part1 = whole.astype(jnp.bfloat16)
            rest = whole - part1.astype(jnp.float32)
            part2 = rest.astype(jnp.bfloat16)
            part3 = (rest - part2.astype(jnp.float32)).astype(jnp.bfloat16)
            out_ref[ROWS:, mine] = jnp.concatenate(
                [part1, part2, part3, jnp.zeros((8, HEAD), jnp.bfloat16)], axis=0
            )
            logs = []


def attend(queries, sources, state=None, final=False, heads=(0, 1, 2)):
    whole = pl.BlockSpec(memory_space=pltpu.VMEM)
    operands, places = [queries], []
    for source in sources:
        place = []
        for array, first in (source[:2], source[2:]):
            known = [i for i, operand in enumerate(operands) if operand is array and i > 0]
            if not known:
                operands.append(array)
            place.append((known[0] if known else len(operands) - 1, first))
        places.append(place)
    if state is not None:
        operands.append(state)
    if final:
        out_shape = jax.ShapeDtypeStruct((SENT_ROWS, len(heads) * HEAD), jnp.bfloat16)
    else:
        out_shape = jax.ShapeDtypeStruct((len(heads), ROWS, 3 * HEAD), jnp.float32)
    return pl.pallas_call(
        functools.partial(
            attend_kernel,
            heads=heads,
            places=places,
            resumed=state is not None,
            final=final,
        ),
        in_specs=[whole] * len(operands),
        out_specs=whole,
        out_shape=out_shape,
        compiler_params=pltpu.CompilerParams(vmem_limit_bytes=VMEM),
        cost_estimate=pl.CostEstimate(flops=1, bytes_accessed=1, transcendentals=0),
    )(*operands)


def merge_kernel(mine_ref, most_ref, rest_ref, out_ref):
    eye = diagonal()
    ones = jnp.ones((2 * HEAD, HEAD), jnp.bfloat16)
    for h in range(HEADS_HERE):
        back_ref, place = (rest_ref, 0) if h == 2 else (most_ref, h)
        parts = [
            (mine_ref, slice(h * HEAD, (h + 1) * HEAD)),
            (back_ref, slice(place * HEAD, (place + 1) * HEAD)),
        ]
        logs = []
        for part, at in parts:
            stats = part[ROWS:, at].astype(jnp.float32)
            logs.append(stats[0:8] + (stats[8:16] + stats[16:24]))
        high = functools.reduce(jnp.maximum, logs)
        shares = [jnp.exp2(log - high) for log in logs]
        whole = functools.reduce(jnp.add, shares)
        shares = [share / whole for share in shares]
        for g in range(ROWS // HEAD):
            rows = slice(g * HEAD, (g + 1) * HEAD)
            total = None
            for (part, at), share in zip(parts, shares):
                spread = jnp.where(eye, share[g : g + 1, :], 0.0)
                coarse = spread.astype(jnp.bfloat16)
                fine = (spread - coarse.astype(jnp.float32)).astype(jnp.bfloat16)
                column = jnp.dot(
                    jnp.concatenate([coarse, fine], axis=1),
                    ones,
                    preferred_element_type=jnp.float32,
                )
                term = part[rows, at].astype(jnp.float32) * column
                total = term if total is None else total + term
            out_ref[rows, h * HEAD : (h + 1) * HEAD] = total.astype(out_ref.dtype)


def merge(parts):
    return pl.pallas_call(
        merge_kernel,
        in_specs=[pl.BlockSpec(memory_space=pltpu.VMEM)] * len(parts),
        out_specs=pl.BlockSpec(memory_space=pltpu.VMEM),
        out_shape=jax.ShapeDtypeStruct((ROWS, WIDTH), jnp.bfloat16),
        compiler_params=pltpu.CompilerParams(vmem_limit_bytes=VMEM),
        cost_estimate=pl.CostEstimate(flops=1, bytes_accessed=1, transcendentals=0),
    )(*parts)


def swap(array, axis):
    pairs = {"c": [(0, 1)], "xl": [(0, 1)], "y01": [(0, 1), (2, 3)], "y12": [(1, 2), (3, 0)]}[axis]
    both = pairs + [(j, i) for i, j in pairs]
    return lax.ppermute(array, axis[0] if axis[0] == "y" else axis, both)


def after(first, *rest):
    return lax.optimization_barrier((first, *rest))


def per_device(queries, key_states, value_states):
    grouped_kv = regroup(key_states[0], value_states[0])
    own_kv = lax.all_to_all(grouped_kv, ULY, 0, 0).reshape(ROWS, 2 * WIDTH)
    own_kv, queries = after(own_kv, queries)
    next_kv = swap(own_kv, "y01")
    side_kv = swap(own_kv, "y12")
    core_kv = swap(own_kv, "c")
    both_q = lax.all_to_all(copy_out(queries[0]), ("z", "xh", "xl"), 0, 0)
    own_q, far_q = part(both_q)

    def whole(array):
        return (array, 0, array, WIDTH)

    near = [whole(own_kv), whole(core_kv)]
    state_far = attend(far_q, near)
    side_kv, next_kv, state_far = after(side_kv, next_kv, state_far)
    side_core_kv = swap(side_kv, "c")
    next_core_kv = swap(next_kv, "c")
    diagonal_k = swap(next_kv[:, :WIDTH], "y12")
    diagonal_v = swap(side_kv[:, WIDTH:], "y01")

    around = [whole(side_kv), whole(side_core_kv), whole(next_kv), whole(next_core_kv)]
    own_q, state_far = after(own_q, state_far)
    state_own = attend(own_q, near)
    state_far, state_own = after(state_far, state_own)
    state_far = attend(far_q, around, state_far)
    state_far, diagonal_k, diagonal_v = after(state_far, diagonal_k, diagonal_v)
    diagonal_core_k = swap(diagonal_k, "c")
    diagonal_core_v = swap(diagonal_v, "c")
    diagonal = (diagonal_k, 0, diagonal_v, 0)
    diagonal_core = (diagonal_core_k, 0, diagonal_core_v, 0)
    state_far = attend(far_q, [diagonal], state_far)
    most = attend(far_q, [diagonal_core], state_far, final=True, heads=(0, 1))
    most, state_far = after(most, state_far)
    back_most = swap(most, "xl")
    rest = attend(far_q, [diagonal_core], state_far, final=True, heads=(2,))
    back_rest = swap(rest, "xl")
    mine = attend(own_q, around + [diagonal, diagonal_core], state_own, final=True)

    merged = merge([mine, back_most, back_rest]).reshape(GROUPS, TOKENS, WIDTH)
    return ungroup(lax.all_to_all(merged, ULY, 0, 0))[None]


def solution(mesh):
    split = Mesh(mesh.devices.reshape(4, 2, 2, 4, 2), ("z", "xh", "xl", "y", "c"))
    placed = P(None, ("z", "xh", "xl", "y", "c"), None)
    return jax.shard_map(
        per_device,
        mesh=split,
        in_specs=(placed, placed, placed),
        out_specs=placed,
        check_vma=False,
    )
```

```python
import functools
import math

import jax
import jax.numpy as jnp
from jax import lax
from jax.experimental import pallas as pl
from jax.experimental.pallas import tpu as pltpu
from jax.sharding import Mesh
from jax.sharding import PartitionSpec as P

HEAD = 128
HEADS_HERE = 3
WIDTH = HEAD * HEADS_HERE
GROUPS = 8
TOKENS = 96
ROWS = GROUPS * TOKENS
STAT_ROWS = 32
SENT_ROWS = ROWS + STAT_ROWS
SUB_ROWS = 256
SCALE = math.log2(math.e) / math.sqrt(HEAD)
ULY = ("z", "xh")
VMEM = 20 * 2**20
WHOLE_VMEM = 60 * 2**20


def regroup_kernel(*refs):
    count = (len(refs) - 2) // 2
    in_refs, out_ref, held, sems = refs[:count], refs[count], refs[count + 1 : -1], refs[-1]
    half = TOKENS // 2
    copies = [
        pltpu.make_async_copy(
            ref.at[side * half : (side + 1) * half],
            block.at[side * half : (side + 1) * half],
            sems.at[part, side],
        )
        for part, (ref, block) in enumerate(zip(in_refs, held))
        for side in range(2)
    ]
    for n, copy in enumerate(copies):
        copy.start(priority=n % 2)
    for part, block in enumerate(held):
        copies[2 * part].wait()
        copies[2 * part + 1].wait()
        for g in range(GROUPS):
            out_ref[g, :, part * WIDTH : (part + 1) * WIDTH] = block[:, g * WIDTH : (g + 1) * WIDTH]


def regroup(*arrays):
    return pl.pallas_call(
        regroup_kernel,
        in_specs=[pl.BlockSpec(memory_space=pl.ANY)] * len(arrays),
        out_specs=pl.BlockSpec(memory_space=pltpu.VMEM),
        out_shape=jax.ShapeDtypeStruct((GROUPS, TOKENS, len(arrays) * WIDTH), arrays[0].dtype),
        scratch_shapes=[pltpu.VMEM(array.shape, array.dtype) for array in arrays]
        + [pltpu.SemaphoreType.DMA((len(arrays), 2))],
        compiler_params=pltpu.CompilerParams(vmem_limit_bytes=WHOLE_VMEM),
    )(*arrays)


def copy_out_kernel(in_ref, out_ref, held, sem):
    copy = pltpu.make_async_copy(in_ref, held, sem)
    copy.start()
    copy.wait()
    for g in range(GROUPS):
        for x in range(2):
            out_ref[2 * g + x] = held[:, g * WIDTH : (g + 1) * WIDTH]


def copy_out(queries):
    return pl.pallas_call(
        copy_out_kernel,
        in_specs=[pl.BlockSpec(memory_space=pl.ANY)],
        out_specs=pl.BlockSpec(memory_space=pltpu.VMEM),
        out_shape=jax.ShapeDtypeStruct((2 * GROUPS, TOKENS, WIDTH), queries.dtype),
        scratch_shapes=[pltpu.VMEM(queries.shape, queries.dtype), pltpu.SemaphoreType.DMA],
        compiler_params=pltpu.CompilerParams(vmem_limit_bytes=VMEM),
    )(queries)


def part_kernel(in_ref, own_ref, far_ref):
    own = lax.axis_index("xl")
    for g in range(GROUPS):
        at = slice(g * TOKENS, (g + 1) * TOKENS)
        own_ref[at, :] = in_ref[2 * g + own]
        far_ref[at, :] = in_ref[2 * g + 1 - own]


def part(both):
    whole = pl.BlockSpec(memory_space=pltpu.VMEM)
    return pl.pallas_call(
        part_kernel,
        in_specs=[whole],
        out_specs=[whole, whole],
        out_shape=[jax.ShapeDtypeStruct((ROWS, WIDTH), both.dtype)] * 2,
        compiler_params=pltpu.CompilerParams(vmem_limit_bytes=VMEM),
        cost_estimate=pl.CostEstimate(flops=1, bytes_accessed=1, transcendentals=0),
    )(both)


def ungroup_kernel(in_ref, out_ref):
    for g in range(GROUPS):
        out_ref[:, g * WIDTH : (g + 1) * WIDTH] = in_ref[g]


def ungroup(parts):
    whole = pl.BlockSpec(memory_space=pltpu.VMEM)
    return pl.pallas_call(
        ungroup_kernel,
        in_specs=[whole],
        out_specs=whole,
        out_shape=jax.ShapeDtypeStruct((TOKENS, GROUPS * WIDTH), parts.dtype),
        compiler_params=pltpu.CompilerParams(vmem_limit_bytes=VMEM),
    )(parts)


def diagonal():
    rows = lax.broadcasted_iota(jnp.int32, (HEAD, HEAD), 0)
    cols = lax.broadcasted_iota(jnp.int32, (HEAD, HEAD), 1)
    return rows == cols


def across(column, width):
    return jnp.concatenate([column] * (width // HEAD), axis=1)


def attend_kernel(*refs, heads, places, resumed, final):
    q_ref = refs[0]
    sources = len(places)
    state_ref = refs[-2] if resumed else None
    out_ref = refs[-1]
    tiles = ROWS // SUB_ROWS
    jobs = [(h, t, s) for h in heads for t in range(tiles) for s in range(sources)]
    ones = jnp.ones((ROWS, HEAD), jnp.bfloat16)

    def columns(s, which, h):
        ref, first = places[s][which]
        at = first + h * HEAD
        return refs[ref][:, at : at + HEAD]

    def scores_of(h, t, s):
        return lax.dot_general(
            q_ref[t * SUB_ROWS : (t + 1) * SUB_ROWS, h * HEAD : (h + 1) * HEAD],
            columns(s, 0, h),
            (((1,), (1,)), ((), ())),
            preferred_element_type=jnp.float32,
        )

    top = total = None
    logs = []
    scores = scores_of(*jobs[0])
    for n, (h, t, s) in enumerate(jobs):
        upcoming = scores_of(*jobs[n + 1]) if n + 1 < len(jobs) else None
        at = slice(t * SUB_ROWS, (t + 1) * SUB_ROWS)
        place = h - heads[0]
        mine = slice(place * HEAD, (place + 1) * HEAD)
        if s == 0 and resumed:
            total = state_ref[h, at, : 2 * HEAD]
            top = state_ref[h, at, 2 * HEAD :]
        first = s == 0 and not resumed
        high = jnp.max(scores, axis=1, keepdims=True) * SCALE
        high = jnp.broadcast_to(high, (SUB_ROWS, HEAD))
        if not first:
            high = jnp.maximum(top, high)
        weights = jnp.exp2(scores * SCALE - across(high, ROWS)).astype(jnp.bfloat16)
        widened = jnp.concatenate([columns(s, 1, h), ones], axis=1)
        product = jnp.dot(weights, widened, preferred_element_type=jnp.float32)
        if not first:
            product = product + total * across(jnp.exp2(top - high), 2 * HEAD)
        top, total = high, product
        if s == sources - 1:
            if final:
                row_sum = total[:, HEAD:]
                out_ref[at, mine] = (total[:, :HEAD] / row_sum).astype(out_ref.dtype)
                logs.append(top + jnp.log2(row_sum))
            else:
                out_ref[place, at, : 2 * HEAD] = total
                out_ref[place, at, 2 * HEAD :] = top
        scores = upcoming
        if final and s == sources - 1 and t == tiles - 1:
            eye = diagonal()
            lines = []
            for log in logs:
                for g in range(SUB_ROWS // HEAD):
                    piece = log[g * HEAD : (g + 1) * HEAD]
                    lines.append(jnp.sum(jnp.where(eye, piece, 0.0), axis=0, keepdims=True))
            lines.append(jnp.zeros((8 - len(lines), HEAD), jnp.float32))
            whole = jnp.concatenate(lines, axis=0)
            part1 = whole.astype(jnp.bfloat16)
            rest = whole - part1.astype(jnp.float32)
            part2 = rest.astype(jnp.bfloat16)
            part3 = (rest - part2.astype(jnp.float32)).astype(jnp.bfloat16)
            out_ref[ROWS:, mine] = jnp.concatenate(
                [part1, part2, part3, jnp.zeros((8, HEAD), jnp.bfloat16)], axis=0
            )
            logs = []


def attend(queries, sources, state=None, final=False, heads=(0, 1, 2)):
    whole = pl.BlockSpec(memory_space=pltpu.VMEM)
    operands, places = [queries], []
    for source in sources:
        place = []
        for array, first in (source[:2], source[2:]):
            known = [i for i, operand in enumerate(operands) if operand is array and i > 0]
            if not known:
                operands.append(array)
            place.append((known[0] if known else len(operands) - 1, first))
        places.append(place)
    if state is not None:
        operands.append(state)
    if final:
        out_shape = jax.ShapeDtypeStruct((SENT_ROWS, len(heads) * HEAD), jnp.bfloat16)
    else:
        out_shape = jax.ShapeDtypeStruct((len(heads), ROWS, 3 * HEAD), jnp.float32)
    return pl.pallas_call(
        functools.partial(
            attend_kernel,
            heads=heads,
            places=places,
            resumed=state is not None,
            final=final,
        ),
        in_specs=[whole] * len(operands),
        out_specs=whole,
        out_shape=out_shape,
        compiler_params=pltpu.CompilerParams(vmem_limit_bytes=VMEM),
        cost_estimate=pl.CostEstimate(flops=1, bytes_accessed=1, transcendentals=0),
    )(*operands)


def merge_kernel(mine_ref, most_ref, rest_ref, out_ref):
    eye = diagonal()
    ones = jnp.ones((2 * HEAD, HEAD), jnp.bfloat16)
    for h in range(HEADS_HERE):
        back_ref, place = (rest_ref, 0) if h == 2 else (most_ref, h)
        parts = [
            (mine_ref, slice(h * HEAD, (h + 1) * HEAD)),
            (back_ref, slice(place * HEAD, (place + 1) * HEAD)),
        ]
        logs = []
        for part, at in parts:
            stats = part[ROWS:, at].astype(jnp.float32)
            logs.append(stats[0:8] + (stats[8:16] + stats[16:24]))
        high = functools.reduce(jnp.maximum, logs)
        shares = [jnp.exp2(log - high) for log in logs]
        whole = functools.reduce(jnp.add, shares)
        shares = [share / whole for share in shares]
        for g in range(ROWS // HEAD):
            rows = slice(g * HEAD, (g + 1) * HEAD)
            total = None
            for (part, at), share in zip(parts, shares):
                spread = jnp.where(eye, share[g : g + 1, :], 0.0)
                coarse = spread.astype(jnp.bfloat16)
                fine = (spread - coarse.astype(jnp.float32)).astype(jnp.bfloat16)
                column = jnp.dot(
                    jnp.concatenate([coarse, fine], axis=1),
                    ones,
                    preferred_element_type=jnp.float32,
                )
                term = part[rows, at].astype(jnp.float32) * column
                total = term if total is None else total + term
            out_ref[rows, h * HEAD : (h + 1) * HEAD] = total.astype(out_ref.dtype)


def merge(parts):
    return pl.pallas_call(
        merge_kernel,
        in_specs=[pl.BlockSpec(memory_space=pltpu.VMEM)] * len(parts),
        out_specs=pl.BlockSpec(memory_space=pltpu.VMEM),
        out_shape=jax.ShapeDtypeStruct((ROWS, WIDTH), jnp.bfloat16),
        compiler_params=pltpu.CompilerParams(vmem_limit_bytes=VMEM),
        cost_estimate=pl.CostEstimate(flops=1, bytes_accessed=1, transcendentals=0),
    )(*parts)


def swap(array, axis):
    pairs = {"c": [(0, 1)], "xl": [(0, 1)], "y01": [(0, 1), (2, 3)], "y12": [(1, 2), (3, 0)]}[axis]
    both = pairs + [(j, i) for i, j in pairs]
    return lax.ppermute(array, axis[0] if axis[0] == "y" else axis, both)


def after(first, *rest):
    return lax.optimization_barrier((first, *rest))


def per_device(queries, key_states, value_states):
    grouped_kv = regroup(key_states[0], value_states[0])
    own_kv = lax.all_to_all(grouped_kv, ULY, 0, 0).reshape(ROWS, 2 * WIDTH)
    own_kv, queries = after(own_kv, queries)
    next_kv = swap(own_kv, "y01")
    side_kv = swap(own_kv, "y12")
    core_kv = swap(own_kv, "c")
    both_q = lax.all_to_all(copy_out(queries[0]), ("z", "xh", "xl"), 0, 0)
    own_q, far_q = part(both_q)

    def whole(array):
        return (array, 0, array, WIDTH)

    near = [whole(own_kv), whole(core_kv)]
    state_far = attend(far_q, near)
    side_kv, next_kv, state_far = after(side_kv, next_kv, state_far)
    side_core_kv = swap(side_kv, "c")
    next_core_kv = swap(next_kv, "c")
    diagonal_k = swap(next_kv[:, :WIDTH], "y12")
    diagonal_v = swap(side_kv[:, WIDTH:], "y01")

    around = [whole(side_kv), whole(side_core_kv), whole(next_kv), whole(next_core_kv)]
    own_q, state_far = after(own_q, state_far)
    state_own = attend(own_q, near)
    state_far, state_own = after(state_far, state_own)
    state_far = attend(far_q, around, state_far)
    state_far, diagonal_k, diagonal_v = after(state_far, diagonal_k, diagonal_v)
    diagonal_core_k = swap(diagonal_k, "c")
    diagonal_core_v = swap(diagonal_v, "c")
    diagonal = (diagonal_k, 0, diagonal_v, 0)
    diagonal_core = (diagonal_core_k, 0, diagonal_core_v, 0)
    state_far = attend(far_q, [diagonal], state_far)
    most = attend(far_q, [diagonal_core], state_far, final=True, heads=(0, 1))
    most, state_far = after(most, state_far)
    back_most = swap(most, "xl")
    rest = attend(far_q, [diagonal_core], state_far, final=True, heads=(2,))
    back_rest = swap(rest, "xl")
    mine = attend(own_q, around + [diagonal, diagonal_core], state_own, final=True)

    merged = merge([mine, back_most, back_rest]).reshape(GROUPS, TOKENS, WIDTH)
    return ungroup(lax.all_to_all(merged, ULY, 0, 0))[None]


def solution(mesh):
    split = Mesh(mesh.devices.reshape(4, 2, 2, 4, 2), ("z", "xh", "xl", "y", "c"))
    placed = P(None, ("z", "xh", "xl", "y", "c"), None)
    return jax.shard_map(
        per_device,
        mesh=split,
        in_specs=(placed, placed, placed),
        out_specs=placed,
        check_vma=False,
    )
```
